32 devices in a mesh: px: 8 (over z, x), py: 4 (over y, core).
Axes of the slice: x: 2, y: 2, z: 4, core: 2. Of those that a mesh axis runs over, the one named last changes fastest.
Arguments:
- rho_hat: float32 [2, 128, 768, 768], P(None, 'px', 'py'), may hold values from -6 to 6
Outputs:
- v_hat: float32 [2, 128, 768, 768], P(None, 'px', 'py')
The draws below stay inside these ranges and needn't reach their ends.
All inputs are finite; a program needn't handle non-finite values.
Results may differ from the reference program's by a relative error of at most 0.0003.
Values sent between devices are 32-bit elements; how exact they have to be, the bound alone decides.
A program may use at most 192 MiB of HBM per device.

```python
import math
import jax
import jax.numpy as jnp

NX = 768
NY = 768
NZ = 128


def block_scale(key, extent, shards, low, top_value):
    factor_of = 1.0
    for axis_at, shards_of in shards:
        draws = jax.random.uniform(jax.random.fold_in(jax.random.fold_in(key, 6), axis_at), (shards_of,), jnp.float32, low / len(shards), top_value / len(shards))
        factor_of = factor_of * jnp.repeat(jnp.exp(draws), extent[axis_at] // shards_of).reshape((-1,) + (1,) * (len(extent) - 1 - axis_at))
    return factor_of


def gaussian(rng, shape, scale, most, split=(), kind=jnp.bfloat16):
    array = jax.random.normal(rng, shape, jnp.float32) * scale
    if len(split) > 0:
        array = block_scale(rng, shape, split, -0.22, 0.18) * array
    return jnp.clip(array, min=-most, max=most).astype(kind)


def setup_inputs(seed: int = 0) -> dict:
    seeds = jax.random.split(jax.random.key(seed), 2)
    return {
        "rho_hat": gaussian(seeds[0], (2, NZ, NX, NY), 1.0, 6.0, ((1, 8), (2, 4)), jnp.float32),
    }


grid_step = 0.25
density_floor = 0.02
density_scale = 0.2
kappa_value = 0.804
mu_value = 0.2195149727645171
beta_value = 0.06672455060314922
gamma_value = (1.0 - math.log(2.0)) / (math.pi * math.pi)
correlation_scale = 0.031091
correlation_alpha = 0.2137
correlation_terms = (7.5957, 3.5876, 1.6382, 0.49294)

def energy_density(rho, sigma):
    cube = jnp.cbrt(rho)
    k_fermi = (3.0 * math.pi * math.pi) ** (1.0 / 3.0) * cube
    exchange_unif = -0.75 * (3.0 / math.pi) ** (1.0 / 3.0) * cube * rho
    s_square = sigma / (4.0 * k_fermi * k_fermi * rho * rho)
    enhance = 1.0 + kappa_value - kappa_value / (1.0 + mu_value * s_square / kappa_value)
    radius = (3.0 / (4.0 * math.pi)) ** (1.0 / 3.0) / cube
    root = jnp.sqrt(radius)
    denom = 2.0 * correlation_scale * (correlation_terms[0] * root + correlation_terms[1] * radius + correlation_terms[2] * radius * root + correlation_terms[3] * radius * radius)
    uniform_corr = -2.0 * correlation_scale * (1.0 + correlation_alpha * radius) * jnp.log(1.0 + 1.0 / denom)
    screen_square = 4.0 * k_fermi / math.pi
    t_square = sigma / (4.0 * screen_square * rho * rho)
    coefficient = beta_value / gamma_value / (jnp.exp(-uniform_corr / gamma_value) - 1.0)
    scaled = coefficient * t_square
    gradient_term = gamma_value * jnp.log(1.0 + beta_value / gamma_value * t_square * (1.0 + scaled) / (1.0 + scaled + scaled * scaled))
    return exchange_unif * enhance + rho * (uniform_corr + gradient_term)

def clamp_depth(field):
    return jnp.concatenate([field[:1], field, field[-1:]], axis=0)

def smooth_depth(field):
    padded = clamp_depth(field)
    return 0.25 * padded[:-2] + 0.5 * padded[1:-1] + 0.25 * padded[2:]

def slope_depth(field):
    padded = clamp_depth(field)
    return (padded[2:] - padded[:-2]) / (2.0 * grid_step)

def roll_smooth(field, axis):
    return 0.25 * jnp.roll(field, 1, axis) + 0.5 * field + 0.25 * jnp.roll(field, -1, axis)

def roll_slope(field, axis):
    return (jnp.roll(field, -1, axis) - jnp.roll(field, 1, axis)) / (2.0 * grid_step)

def reference(rho_hat):
    spectrum = rho_hat[0] + 1j * rho_hat[1]
    field = jnp.real(jnp.fft.ifft2(spectrum, axes=(1, 2))) * math.sqrt(NX * NY)
    density = density_floor + density_scale * jax.nn.softplus(field)
    smooth = smooth_depth(roll_smooth(roll_smooth(density, 1), 2))
    grad_x = roll_slope(smooth, 1)
    grad_y = roll_slope(smooth, 2)
    grad_z = slope_depth(smooth)
    sigma = grad_x * grad_x + grad_y * grad_y + grad_z * grad_z
    energy, pullback = jax.vjp(energy_density, smooth, sigma)
    d_rho, d_sigma = pullback(jnp.ones_like(energy))
    flux_x = 2.0 * d_sigma * grad_x
    flux_y = 2.0 * d_sigma * grad_y
    flux_z = 2.0 * d_sigma * grad_z
    spread = roll_slope(flux_x, 1) + roll_slope(flux_y, 2) + slope_depth(flux_z)
    potential = d_rho - spread
    result = jnp.fft.fft2(potential, axes=(1, 2)) / math.sqrt(NX * NY)
    result = result.at[:, 0, 0].set(0.0)
    return jnp.stack([jnp.real(result), jnp.imag(result)], axis=0).astype(rho_hat.dtype)
```

```python
import functools
import math

import jax
import jax.numpy as jnp
import numpy as np
from jax import lax
from jax.experimental import pallas as pl
from jax.experimental.pallas import tpu as pltpu
from jax.sharding import PartitionSpec as P

grid_step = 0.25
density_floor = 0.02
density_scale = 0.2
kappa_value = 0.804
mu_value = 0.2195149727645171
beta_value = 0.06672455060314922
gamma_value = (1.0 - math.log(2.0)) / (math.pi * math.pi)
correlation_scale = 0.031091
correlation_alpha = 0.2137
correlation_terms = (7.5957, 3.5876, 1.6382, 0.49294)
plane_offset = -0.55
rim_y = 4
rim_z = 3


def point_terms(rho, sigma):
    log_rho = jnp.log(rho)
    sixth = jnp.exp(log_rho * (-1.0 / 6.0))
    inv = sixth * sixth
    inv2 = inv * inv
    inv4 = inv2 * inv2
    cube = rho * inv2
    s_coef = 1.0 / (4.0 * (3.0 * math.pi**2) ** (2.0 / 3.0))
    t_coef = math.pi / (16.0 * (3.0 * math.pi**2) ** (1.0 / 3.0))
    x_coef = -0.75 * (3.0 / math.pi) ** (1.0 / 3.0)
    s_per = s_coef * (inv4 * inv4)
    s_square = sigma * s_per
    quot = 1.0 / (1.0 + (mu_value / kappa_value) * s_square)
    slope = mu_value * quot * quot
    enhance = (1.0 + kappa_value) - kappa_value * quot
    x_cube = x_coef * cube
    exch_rho = (4.0 / 3.0) * x_cube * (enhance - 2.0 * slope * s_square)
    exch_sigma = x_cube * rho * slope * s_per
    r_coef = (3.0 / (4.0 * math.pi)) ** (1.0 / 3.0)
    radius = r_coef * inv
    root = math.sqrt(r_coef) * sixth
    b1, b2, b3, b4 = (2.0 * correlation_scale * b for b in correlation_terms)
    denom = root * (b1 + b3 * radius) + radius * (b2 + b4 * radius)
    r_denom = root * (0.5 * b1 + 1.5 * b3 * radius) + radius * (b2 + 2.0 * b4 * radius)
    pair = 1.0 / (denom * (denom + 1.0))
    logs = jnp.log(1.0 + (denom + 1.0) * pair)
    lead = 1.0 + correlation_alpha * radius
    corr = (-2.0 * correlation_scale) * lead * logs
    r_corr = (2.0 * correlation_scale) * (
        lead * r_denom * pair - correlation_alpha * radius * logs
    )
    t_per = t_coef * (inv4 * inv2 * inv)
    t_square = sigma * t_per
    less = 1.0 / (jnp.exp(corr * (-1.0 / gamma_value)) - 1.0)
    coefficient = (beta_value / gamma_value) * less
    scaled = coefficient * t_square
    bottom = 1.0 / (1.0 + scaled + scaled * scaled)
    ratio = (1.0 + scaled) * bottom
    ratio_slope = -scaled * (2.0 + scaled) * bottom * bottom
    arg = 1.0 + (beta_value / gamma_value) * t_square * ratio
    front = beta_value / arg
    h_value = gamma_value * jnp.log(arg)
    h_t = front * (ratio + scaled * ratio_slope)
    h_corr = front * t_square * ratio_slope * scaled * (1.0 + less) * (1.0 / gamma_value)
    corr_rho = (
        corr + h_value - (1.0 / 3.0) * r_corr * (1.0 + h_corr) - (7.0 / 3.0) * t_square * h_t
    )
    corr_sigma = rho * h_t * t_per
    return exch_rho + corr_rho, exch_sigma + corr_sigma


def local_kernel(planes, edge_ref, field_ref, out_ref, flat, smooth, flux_z, part, gx, gy, fy):
    step = pl.program_id(0)
    rows, cols = gx.shape
    strips = rows // 8
    half = 1.0 / (2.0 * grid_step)
    low = edge_ref[0] == 1
    high = edge_ref[1] == 1

    def roll(cells, amount, axis):
        return pltpu.roll(cells, amount % cells.shape[axis], axis)

    @pl.loop(0, strips)
    def _(i):
        at = pl.ds(pl.multiple_of(i * 8, 8), 8)
        field = field_ref[0, at, :]
        soft = jnp.maximum(field, 0.0) + jnp.log(1.0 + jnp.exp(-jnp.abs(field)))
        density = density_floor + density_scale * soft
        gx[at, :] = 0.5 * density + 0.25 * (roll(density, 1, 1) + roll(density, -1, 1))

    across = gx[...]
    flat[lax.rem(step, 3)] = 0.5 * across + 0.25 * (roll(across, 1, 0) + roll(across, -1, 0))

    @pl.when(step >= 2)
    def _():
        smooth[lax.rem(step + 2, 3)] = 0.5 * flat[lax.rem(step + 2, 3)] + 0.25 * (
            flat[lax.rem(step + 1, 3)] + flat[lax.rem(step, 3)]
        )

    @pl.when((step == 5) & low)
    def _():
        smooth[lax.rem(step, 3)] = smooth[lax.rem(step + 1, 3)]

    @pl.when((step == planes + 4) & high)
    def _():
        smooth[lax.rem(step + 2, 3)] = smooth[lax.rem(step + 1, 3)]

    @pl.when(step >= 4)
    def _():
        before = lax.rem(step, 3)
        here = lax.rem(step + 1, 3)
        after = lax.rem(step + 2, 3)
        center = smooth[here]
        gy[...] = (roll(center, -1, 0) - roll(center, 1, 0)) * half
        now = lax.rem(step + 1, 3)
        slot = lax.rem(step, 2)

        @pl.loop(0, strips)
        def _(i):
            at = pl.ds(pl.multiple_of(i * 8, 8), 8)
            rho = smooth[here, at, :]
            grad_x = (roll(rho, -1, 1) - roll(rho, 1, 1)) * half
            grad_y = gy[at, :]
            grad_z = (smooth[after, at, :] - smooth[before, at, :]) * half
            sigma = grad_x * grad_x + grad_y * grad_y + grad_z * grad_z
            d_rho, d_sigma = point_terms(rho, sigma)
            twice = 2.0 * d_sigma
            flux_x = twice * grad_x
            fy[at, :] = twice * grad_y
            flux_z[now, at, :] = twice * grad_z
            part[slot, at, :] = (d_rho - plane_offset) - (
                roll(flux_x, -1, 1) - roll(flux_x, 1, 1)
            ) * half

        flux_y = fy[...]
        part[slot] = part[slot] - (roll(flux_y, -1, 0) - roll(flux_y, 1, 0)) * half

    @pl.when((step == 5) & low)
    def _():
        flux_z[lax.rem(step, 3)] = flux_z[lax.rem(step + 1, 3)]

    @pl.when((step == planes + 5) & high)
    def _():
        flux_z[lax.rem(step + 1, 3)] = flux_z[lax.rem(step, 3)]

    @pl.when(step >= 6)
    def _():
        inner = pl.ds(rim_y, rows - 2 * rim_y)
        spread = (flux_z[lax.rem(step + 1, 3)] - flux_z[lax.rem(step + 2, 3)]) * half
        gx[...] = part[lax.rem(step + 1, 2)] - spread
        out_ref[0] = gx[inner, :]


def local_potential(field, edges):
    planes = field.shape[0] - 2 * rim_z
    rows, cols = field.shape[1:]
    plane = pltpu.VMEM((rows, cols), jnp.float32)
    return pl.pallas_call(
        functools.partial(local_kernel, planes),
        grid=(planes + 2 * rim_z,),
        in_specs=[
            pl.BlockSpec(memory_space=pltpu.SMEM),
            pl.BlockSpec((1, rows, cols), lambda p: (p, 0, 0)),
        ],
        out_specs=pl.BlockSpec(
            (1, rows - 2 * rim_y, cols), lambda p: (jnp.maximum(p - 2 * rim_z, 0), 0, 0)
        ),
        out_shape=jax.ShapeDtypeStruct((planes, rows - 2 * rim_y, cols), jnp.float32),
        scratch_shapes=[
            pltpu.VMEM((3, rows, cols), jnp.float32),
            pltpu.VMEM((3, rows, cols), jnp.float32),
            pltpu.VMEM((3, rows, cols), jnp.float32),
            pltpu.VMEM((2, rows, cols), jnp.float32),
            plane,
            plane,
            plane,
        ],
        compiler_params=pltpu.CompilerParams(
            dimension_semantics=("arbitrary",), vmem_limit_bytes=32 * 1024 * 1024
        ),
        cost_estimate=pl.CostEstimate(
            flops=200 * field.size, bytes_accessed=8 * field.size, transcendentals=7 * field.size
        ),
    )(edges, field)


def angles(rows, cols, length):
    return (rows[:, None] * cols[None, :] % length) * (2.0 * math.pi / length)


def on_device(count_x, count_y, rho_hat):
    high = lax.Precision.HIGH
    _, depth, local, width_y = rho_hat.shape
    width_x = local * count_y
    rows = width_y // count_y
    steps = 4
    part = depth // steps
    me = lax.axis_index("py")
    waves_y = np.arange(width_y)
    waves_x = np.arange(width_x)
    points = (
        np.arange(count_y)[:, None] * rows + np.arange(-rim_y, rows + rim_y)[None, :]
    ).reshape(-1) % width_y
    angle = angles(points, waves_y, width_y)
    cos, sin = np.cos(angle), np.sin(angle)
    table = np.stack([np.stack([cos, -sin], 1), np.stack([sin, cos], 1)], 1) / math.sqrt(width_y)
    into_rows = jnp.asarray(
        table.reshape(count_y, rows + 2 * rim_y, 2, 2, width_y).transpose(0, 2, 1, 3, 4),
        jnp.float32,
    )
    angle = angles(waves_x, waves_x, width_x)
    cos, sin = np.cos(angle), np.sin(angle)
    into_cols = jnp.asarray(
        (np.stack([cos, -sin], 0) / math.sqrt(width_x))
        .reshape(2, count_y, local, width_x)
        .transpose(1, 0, 2, 3),
        jnp.float32,
    )
    from_cols = jnp.asarray(
        (np.stack([cos, -sin], 1) / math.sqrt(width_x))
        .reshape(width_x, 2, count_y, local)
        .transpose(2, 0, 1, 3),
        jnp.float32,
    )
    angle = angles(waves_y, waves_y, width_y)
    cos, sin = np.cos(angle), np.sin(angle)
    from_rows = jnp.asarray(
        (np.stack([np.stack([cos, -sin], 1), np.stack([sin, cos], 1)], 0) / math.sqrt(width_y))
        .reshape(2, count_y, rows, 2, width_y)
        .transpose(1, 0, 2, 3, 4),
        jnp.float32,
    )

    def pick(stacked, index):
        return lax.dynamic_index_in_dim(stacked, index, 0, keepdims=False)

    partners = [me ^ s for s in range(count_y)]
    into_rows = [pick(into_rows, p) for p in partners]
    into_cols = [pick(into_cols, p).reshape(2 * local, width_x) for p in partners]
    from_cols = [pick(from_cols, p).reshape(width_x, 2 * local) for p in partners]
    from_rows = [pick(from_rows, p) for p in partners]

    def swap(cells, s):
        if s == 0:
            return cells
        return lax.ppermute(cells, "py", [(i, i ^ s) for i in range(count_y)])

    order = list(range(count_y - 1, -1, -1))
    fields = {}
    for chunk in [steps - 1] + list(range(steps - 1)):
        block = rho_hat[:, chunk * part : (chunk + 1) * part]
        total = None
        for s in order:
            half = jnp.einsum("czxk,dyck->zydx", block, into_rows[s], precision=high)
            half = swap(half.reshape(part, rows + 2 * rim_y, 2 * local), s)
            term = jnp.einsum("zyk,kx->zyx", half, into_cols[s], precision=high)
            total = term if total is None else total + term
        fields[chunk] = total

    at_x = lax.axis_index("px")
    first, last = at_x == 0, at_x == count_x - 1
    from_low = lax.ppermute(
        fields[steps - 1][-rim_z:], "px", [(i, i + 1) for i in range(count_x - 1)]
    )
    from_high = lax.ppermute(fields[0][:rim_z], "px", [(i + 1, i) for i in range(count_x - 1)])
    from_low = jnp.where(first, fields[0][:1], from_low)
    from_high = jnp.where(last, fields[steps - 1][-1:], from_high)
    none = jnp.zeros((), jnp.int32)
    split = steps // 2
    ends = [
        (
            jnp.concatenate(
                [from_low] + [fields[i] for i in range(split)] + [fields[split][:rim_z]]
            ),
            jnp.stack([first.astype(jnp.int32), none]),
        ),
        (
            jnp.concatenate(
                [fields[split - 1][-rim_z:]]
                + [fields[i] for i in range(split, steps)]
                + [from_high]
            ),
            jnp.stack([none, last.astype(jnp.int32)]),
        ),
    ]
    spectra = []
    for field, edges in ends:
        potential = local_potential(field, edges)
        for chunk in range(split):
            block = potential[chunk * part : (chunk + 1) * part]
            total = None
            for s in order:
                half = jnp.einsum("zyx,xk->zyk", block, from_cols[s], precision=high)
                half = swap(half, s).reshape(part, rows, 2, local)
                term = jnp.einsum("zycx,cydk->dzxk", half, from_rows[s], precision=high)
                total = term if total is None else total + term
            spectra.append(total)
    spectra = jnp.concatenate(spectra, axis=1)
    wave_x = me * local + jnp.arange(local, dtype=jnp.int32)
    anchor = (wave_x[:, None] == 0) & (jnp.arange(width_y, dtype=jnp.int32)[None, :] == 0)
    return jnp.where(anchor[None, None], jnp.float32(0.0), spectra)


def solution(mesh):
    return jax.shard_map(
        functools.partial(on_device, mesh.shape["px"], mesh.shape["py"]),
        mesh=mesh,
        in_specs=(P(None, "px", "py", None),),
        out_specs=P(None, "px", "py", None),
        check_vma=False,
    )
```

```python
import functools
import math

import jax
import jax.numpy as jnp
import numpy as np
from jax import lax
from jax.experimental import pallas as pl
from jax.experimental.pallas import tpu as pltpu
from jax.sharding import PartitionSpec as P

grid_step = 0.25
density_floor = 0.02
density_scale = 0.2
kappa_value = 0.804
mu_value = 0.2195149727645171
beta_value = 0.06672455060314922
gamma_value = (1.0 - math.log(2.0)) / (math.pi * math.pi)
correlation_scale = 0.031091
correlation_alpha = 0.2137
correlation_terms = (7.5957, 3.5876, 1.6382, 0.49294)
plane_offset = -0.55
rim_y = 4
rim_z = 3


def point_terms(rho, sigma):
    log_rho = jnp.log(rho)
    sixth = jnp.exp(log_rho * (-1.0 / 6.0))
    inv = sixth * sixth
    inv2 = inv * inv
    inv4 = inv2 * inv2
    cube = rho * inv2
    s_coef = 1.0 / (4.0 * (3.0 * math.pi**2) ** (2.0 / 3.0))
    t_coef = math.pi / (16.0 * (3.0 * math.pi**2) ** (1.0 / 3.0))
    x_coef = -0.75 * (3.0 / math.pi) ** (1.0 / 3.0)
    s_per = s_coef * (inv4 * inv4)
    s_square = sigma * s_per
    quot = 1.0 / (1.0 + (mu_value / kappa_value) * s_square)
    slope = mu_value * quot * quot
    enhance = (1.0 + kappa_value) - kappa_value * quot
    x_cube = x_coef * cube
    exch_rho = (4.0 / 3.0) * x_cube * (enhance - 2.0 * slope * s_square)
    exch_sigma = x_cube * rho * slope * s_per
    r_coef = (3.0 / (4.0 * math.pi)) ** (1.0 / 3.0)
    radius = r_coef * inv
    root = math.sqrt(r_coef) * sixth
    b1, b2, b3, b4 = (2.0 * correlation_scale * b for b in correlation_terms)
    denom = root * (b1 + b3 * radius) + radius * (b2 + b4 * radius)
    r_denom = root * (0.5 * b1 + 1.5 * b3 * radius) + radius * (b2 + 2.0 * b4 * radius)
    pair = 1.0 / (denom * (denom + 1.0))
    logs = jnp.log(1.0 + (denom + 1.0) * pair)
    lead = 1.0 + correlation_alpha * radius
    corr = (-2.0 * correlation_scale) * lead * logs
    r_corr = (2.0 * correlation_scale) * (
        lead * r_denom * pair - correlation_alpha * radius * logs
    )
    t_per = t_coef * (inv4 * inv2 * inv)
    t_square = sigma * t_per
    less = 1.0 / (jnp.exp(corr * (-1.0 / gamma_value)) - 1.0)
    coefficient = (beta_value / gamma_value) * less
    scaled = coefficient * t_square
    bottom = 1.0 / (1.0 + scaled + scaled * scaled)
    ratio = (1.0 + scaled) * bottom
    ratio_slope = -scaled * (2.0 + scaled) * bottom * bottom
    arg = 1.0 + (beta_value / gamma_value) * t_square * ratio
    front = beta_value / arg
    h_value = gamma_value * jnp.log(arg)
    h_t = front * (ratio + scaled * ratio_slope)
    h_corr = front * t_square * ratio_slope * scaled * (1.0 + less) * (1.0 / gamma_value)
    corr_rho = (
        corr + h_value - (1.0 / 3.0) * r_corr * (1.0 + h_corr) - (7.0 / 3.0) * t_square * h_t
    )
    corr_sigma = rho * h_t * t_per
    return exch_rho + corr_rho, exch_sigma + corr_sigma


def local_kernel(planes, start, resumed, *refs):
    if resumed:
        edge_ref, field_ref, before_ref, out_ref, state, gx, gy, fy = refs
    else:
        edge_ref, field_ref, out_ref, state, gx, gy, fy = refs
    flat = state.at[pl.ds(0, 3)]
    smooth = state.at[pl.ds(3, 3)]
    flux_z = state.at[pl.ds(6, 3)]
    part = state.at[pl.ds(9, 2)]
    if resumed:

        @pl.when(pl.program_id(0) == 0)
        def _():
            state[...] = before_ref[...]

    step = pl.program_id(0) + start
    rows, cols = gx.shape
    strips = rows // 8
    half = 1.0 / (2.0 * grid_step)
    low = edge_ref[0] == 1
    high = edge_ref[1] == 1

    def roll(cells, amount, axis):
        return pltpu.roll(cells, amount % cells.shape[axis], axis)

    @pl.loop(0, strips)
    def _(i):
        at = pl.ds(pl.multiple_of(i * 8, 8), 8)
        field = field_ref[0, at, :]
        soft = jnp.maximum(field, 0.0) + jnp.log(1.0 + jnp.exp(-jnp.abs(field)))
        density = density_floor + density_scale * soft
        gx[at, :] = 0.5 * density + 0.25 * (roll(density, 1, 1) + roll(density, -1, 1))

    across = gx[...]
    flat[lax.rem(step, 3)] = 0.5 * across + 0.25 * (roll(across, 1, 0) + roll(across, -1, 0))

    @pl.when(step >= 2)
    def _():
        smooth[lax.rem(step + 2, 3)] = 0.5 * flat[lax.rem(step + 2, 3)] + 0.25 * (
            flat[lax.rem(step + 1, 3)] + flat[lax.rem(step, 3)]
        )

    @pl.when((step == 5) & low)
    def _():
        smooth[lax.rem(step, 3)] = smooth[lax.rem(step + 1, 3)]

    @pl.when((step == planes + 4) & high)
    def _():
        smooth[lax.rem(step + 2, 3)] = smooth[lax.rem(step + 1, 3)]

    @pl.when(step >= 4)
    def _():
        before = lax.rem(step, 3)
        here = lax.rem(step + 1, 3)
        after = lax.rem(step + 2, 3)
        center = smooth[here]
        gy[...] = (roll(center, -1, 0) - roll(center, 1, 0)) * half
        now = lax.rem(step + 1, 3)
        slot = lax.rem(step, 2)

        @pl.loop(0, strips)
        def _(i):
            at = pl.ds(pl.multiple_of(i * 8, 8), 8)
            rho = smooth[here, at, :]
            grad_x = (roll(rho, -1, 1) - roll(rho, 1, 1)) * half
            grad_y = gy[at, :]
            grad_z = (smooth[after, at, :] - smooth[before, at, :]) * half
            sigma = grad_x * grad_x + grad_y * grad_y + grad_z * grad_z
            d_rho, d_sigma = point_terms(rho, sigma)
            twice = 2.0 * d_sigma
            flux_x = twice * grad_x
            fy[at, :] = twice * grad_y
            flux_z[now, at, :] = twice * grad_z
            part[slot, at, :] = (d_rho - plane_offset) - (
                roll(flux_x, -1, 1) - roll(flux_x, 1, 1)
            ) * half

        flux_y = fy[...]
        part[slot] = part[slot] - (roll(flux_y, -1, 0) - roll(flux_y, 1, 0)) * half

    @pl.when((step == 5) & low)
    def _():
        flux_z[lax.rem(step, 3)] = flux_z[lax.rem(step + 1, 3)]

    @pl.when((step == planes + 5) & high)
    def _():
        flux_z[lax.rem(step + 1, 3)] = flux_z[lax.rem(step, 3)]

    @pl.when(step >= 6)
    def _():
        inner = pl.ds(rim_y, rows - 2 * rim_y)
        spread = (flux_z[lax.rem(step + 1, 3)] - flux_z[lax.rem(step + 2, 3)]) * half
        gx[...] = part[lax.rem(step + 1, 2)] - spread
        out_ref[0] = gx[inner, :]


def local_potential(depth, start, field, edges, before):
    steps, rows, cols = field.shape
    skipped = max(start - 2 * rim_z, 0)
    planes = start + steps - 2 * rim_z - skipped
    plane = pltpu.VMEM((rows, cols), jnp.float32)
    whole = pl.BlockSpec((11, rows, cols), lambda p: (0, 0, 0))
    resumed = before is not None
    return pl.pallas_call(
        functools.partial(local_kernel, depth, start, resumed),
        grid=(steps,),
        in_specs=[
            pl.BlockSpec(memory_space=pltpu.SMEM),
            pl.BlockSpec((1, rows, cols), lambda p: (p, 0, 0)),
        ]
        + [whole] * resumed,
        out_specs=[
            pl.BlockSpec(
                (1, rows - 2 * rim_y, cols),
                lambda p: (jnp.maximum(p + start - 2 * rim_z, 0) - skipped, 0, 0),
            ),
            whole,
        ],
        out_shape=[
            jax.ShapeDtypeStruct((planes, rows - 2 * rim_y, cols), jnp.float32),
            jax.ShapeDtypeStruct((11, rows, cols), jnp.float32),
        ],
        scratch_shapes=[plane, plane, plane],
        compiler_params=pltpu.CompilerParams(
            dimension_semantics=("arbitrary",), vmem_limit_bytes=48 * 1024 * 1024
        ),
        cost_estimate=pl.CostEstimate(
            flops=200 * field.size, bytes_accessed=8 * field.size, transcendentals=7 * field.size
        ),
    )(edges, field, *([before] if resumed else []))


def rows_kernel(block_ref, high_ref, low_ref, *refs):
    outs, (stack_high, stack_low) = refs[:-2], refs[-2:]
    local, width = block_ref.shape[2:]
    real, imag = block_ref[0, 0], block_ref[1, 0]
    for d, c, value in ((0, 0, real), (0, 1, -imag), (1, 0, imag), (1, 1, real)):
        at = (pl.ds(d * local, local), pl.ds(c * width, width))
        head = value.astype(jnp.bfloat16)
        stack_high[at] = head
        stack_low[at] = (value - head.astype(jnp.float32)).astype(jnp.bfloat16)

    def product(a, b):
        return lax.dot_general(
            a, b, (((1,), (1,)), ((), ())), preferred_element_type=jnp.float32
        )

    head = stack_high[...]
    total = product(low_ref[...], head)
    total = total + product(high_ref[...], stack_low[...])
    total = total + product(high_ref[...], head)
    rows = total.shape[0] // len(outs)
    for s, out_ref in enumerate(outs):
        out_ref[0] = total[s * rows : (s + 1) * rows]


def to_rows(rho_hat, table_high, table_low, at, count, count_y):
    _, _, local, width = rho_hat.shape
    rows = table_high.shape[0] // count_y
    table = pl.BlockSpec(table_high.shape, lambda z: (0, 0))
    return pl.pallas_call(
        rows_kernel,
        grid=(count,),
        in_specs=[
            pl.BlockSpec((2, 1, local, width), lambda z: (0, at + z, 0, 0)),
            table,
            table,
        ],
        out_specs=[pl.BlockSpec((1, rows, 2 * local), lambda z: (z, 0, 0))] * count_y,
        out_shape=[jax.ShapeDtypeStruct((count, rows, 2 * local), jnp.float32)] * count_y,
        scratch_shapes=[pltpu.VMEM((2 * local, 2 * width), jnp.bfloat16)] * 2,
        compiler_params=pltpu.CompilerParams(
            dimension_semantics=("arbitrary",), vmem_limit_bytes=48 * 1024 * 1024
        ),
        cost_estimate=pl.CostEstimate(
            flops=count * 12 * table_high.size * local,
            bytes_accessed=count * 16 * local * width,
            transcendentals=0,
        ),
    )(rho_hat, table_high, table_low)


def angles(rows, cols, length):
    return (rows[:, None] * cols[None, :] % length) * (2.0 * math.pi / length)


def on_device(count_x, count_y, rho_hat):
    high = lax.Precision.HIGH
    _, depth, local, width_y = rho_hat.shape
    width_x = local * count_y
    rows = width_y // count_y
    steps = 4
    part = depth // steps
    me = lax.axis_index("py")
    waves_y = np.arange(width_y)
    waves_x = np.arange(width_x)
    points = (
        np.arange(count_y)[:, None] * rows + np.arange(-rim_y, rows + rim_y)[None, :]
    ).reshape(-1) % width_y
    angle = angles(points, waves_y, width_y)
    cos, sin = np.cos(angle), np.sin(angle)
    table = np.concatenate([cos, sin], 1) / math.sqrt(width_y)
    table = table.reshape(count_y, rows + 2 * rim_y, 2 * width_y).astype(np.float32)
    head = table.astype(jnp.bfloat16)
    rest = (table - head.astype(np.float32)).astype(jnp.bfloat16)
    angle = angles(waves_x, waves_x, width_x)
    cos, sin = np.cos(angle), np.sin(angle)
    into_cols = jnp.asarray(
        (np.stack([cos, -sin], 0) / math.sqrt(width_x))
        .reshape(2, count_y, local, width_x)
        .transpose(1, 0, 2, 3),
        jnp.float32,
    )
    from_cols = jnp.asarray(
        (np.stack([cos, -sin], 1) / math.sqrt(width_x))
        .reshape(width_x, 2, count_y, local)
        .transpose(2, 0, 1, 3),
        jnp.float32,
    )
    angle = angles(waves_y, waves_y, width_y)
    cos, sin = np.cos(angle), np.sin(angle)
    from_rows = jnp.asarray(
        (np.stack([np.stack([cos, -sin], 1), np.stack([sin, cos], 1)], 0) / math.sqrt(width_y))
        .reshape(2, count_y, rows, 2, width_y)
        .transpose(1, 0, 2, 3, 4),
        jnp.float32,
    )

    def pick(stacked, index):
        return lax.dynamic_index_in_dim(stacked, index, 0, keepdims=False)

    partners = [me ^ s for s in range(count_y)]
    table_high = jnp.concatenate([pick(jnp.asarray(head), p) for p in partners])
    table_low = jnp.concatenate([pick(jnp.asarray(rest), p) for p in partners])
    into_cols = [pick(into_cols, p).reshape(2 * local, width_x) for p in partners]
    from_cols = [pick(from_cols, p).reshape(width_x, 2 * local) for p in partners]
    from_rows = [pick(from_rows, p) for p in partners]

    def swap(cells, s):
        if s == 0:
            return cells
        return lax.ppermute(cells, "py", [(i, i ^ s) for i in range(count_y)])

    order = list(range(count_y - 1, -1, -1))
    def after(values, *others):
        return lax.optimization_barrier((values, others))[0]

    halves = {}
    for chunk in [steps - 1] + list(range(steps - 1)):
        halves[chunk] = list(to_rows(rho_hat, table_high, table_low, chunk * part, part, count_y))
        table_low, halves[chunk][0] = lax.optimization_barrier((table_low, halves[chunk][0]))
    arrived = {c: [swap(h, s) for s, h in enumerate(hs)] for c, hs in halves.items()}

    def to_columns(chunk, tables):
        total = None
        for s in order:
            term = jnp.einsum("zyk,kx->zyx", arrived[chunk][s], tables[s], precision=high)
            total = term if total is None else total + term
        return total

    fields = {steps - 1: to_columns(steps - 1, into_cols), 0: to_columns(0, into_cols)}
    at_x = lax.axis_index("px")
    first, last = at_x == 0, at_x == count_x - 1
    from_low = lax.ppermute(
        fields[steps - 1][-rim_z:], "px", [(i, i + 1) for i in range(count_x - 1)]
    )
    from_high = lax.ppermute(fields[0][:rim_z], "px", [(i + 1, i) for i in range(count_x - 1)])
    from_low = jnp.where(first, fields[0][:1], from_low)
    from_high = jnp.where(last, fields[steps - 1][-1:], from_high)
    edges = jnp.stack([first.astype(jnp.int32), last.astype(jnp.int32)])

    def spectral(block):
        return [
            jnp.einsum("zyx,xk->zyk", block, from_cols[s], precision=high) for s in range(count_y)
        ]

    def finish(sent, tables):
        total = None
        for s in order:
            half = sent[s].reshape(-1, rows, 2, local)
            term = jnp.einsum("zycx,cydk->dzxk", half, tables[s], precision=high)
            total = term if total is None else total + term
        return total

    def send(cells):
        return [swap(half, s) for s, half in enumerate(cells)]

    feed = jnp.concatenate([from_low, fields[0]])
    block, state = local_potential(depth, 0, feed, edges, None)
    start = feed.shape[0]
    tables = into_cols
    sent, held = [], block
    for chunk in range(1, steps - 1):
        feed = to_columns(chunk, tables)
        block, state = local_potential(depth, start, feed, edges, state)
        start += part
        if held is not None:
            block, held = jnp.concatenate([held, block]), None
        ready = spectral(block)
        sent.append(send(ready))
        tables = after(into_cols, ready)
        edges = after(edges, ready)
    feed = jnp.concatenate([fields[steps - 1], from_high])
    block, state = local_potential(depth, start, feed, edges, state)
    spectra = [finish(sent[0], from_rows)]
    ready = [spectral(block[:part]), spectral(after(block[part:], spectra[0]))]
    tables = after(from_rows, ready)
    sent += [send(cells) for cells in ready]
    spectra += [finish(cells, tables) for cells in sent[1:]]
    spectra = jnp.concatenate(spectra, axis=1)
    wave_x = me * local + jnp.arange(local, dtype=jnp.int32)
    anchor = (wave_x[:, None] == 0) & (jnp.arange(width_y, dtype=jnp.int32)[None, :] == 0)
    return jnp.where(anchor[None, None], jnp.float32(0.0), spectra)


def solution(mesh):
    return jax.shard_map(
        functools.partial(on_device, mesh.shape["px"], mesh.shape["py"]),
        mesh=mesh,
        in_specs=(P(None, "px", "py", None),),
        out_specs=P(None, "px", "py", None),
        check_vma=False,
    )
```
